32 devices in a mesh: gx: 8 (over z, y), gy: 4 (over x, core).
Axes of the slice: x: 2, y: 2, z: 4, core: 2. Of those that a mesh axis runs over, the one named last changes fastest.
Arguments:
- tracer: float32 [128, 256, 512], P(None, 'gx', 'gy'), may hold values from -11 to 11
- velocity: float32 [2, 256, 512], P(None, 'gx', 'gy'), may hold values from -0.25 to 0.25
- diffusivity: float32 [128], replicated, may hold values from 0.02 to 0.08
- singular: float32 [94], replicated, may hold values from 0.5 to 8
- basis_vectors: float32 [94, 2, 256, 512], P(None, None, 'gx', 'gy'), may hold values from -10 to 10, as said below
Outputs:
- tracer_next: float32 [128, 256, 512], P(None, 'gx', 'gy')
- basis_next: float32 [96, 2, 256, 512], P(None, None, 'gx', 'gy')
The draws below stay inside these ranges and needn't reach their ends.
Inputs may be any that keep to these rules, and one draw needn't show every extreme that they name: The 94 vectors basis_vectors[i], each over all 2 x 256 x 512 cells, are orthogonal with squared length 262144, to float32 rounding.
All inputs are finite; a program needn't handle non-finite values.
Results may differ from the reference program's by a relative error of at most 0.0003.
Values sent between devices are 32-bit elements; how exact they have to be, the bound alone decides.
A program may use at most 64 MiB of HBM per device.

```python
import math
import jax
import jax.numpy as jnp
from jax import lax

NZ = 128
WZ = 2
K = 94
ROOT_ITERS = 5
NX = 256
NY = 512
ROWS = 262144


def joint_draw(key):
    key_noise = jax.random.fold_in(key, 101)
    key_rough = jax.random.fold_in(key, 102)
    key_weights = jax.random.fold_in(key, 103)
    key_mixture = jax.random.fold_in(key, 104)
    position = jnp.arange(NX, dtype=jnp.float32) / NX
    roughness = jax.random.uniform(key_rough, (NX,), jnp.float32, math.log(0.7), math.log(1.4))
    amplitude = 0.6 * jnp.exp(position * math.log(3.0) + roughness)
    noise_part = jax.random.truncated_normal(key_noise, -4.0, 4.0, (NZ, NX, NY), jnp.float32)
    tracer = noise_part * amplitude[None, :, None]
    window = tracer[:WZ].reshape(-1)
    weights = jax.random.normal(key_weights, (K,), jnp.float32)
    mixture = weights[:, None] * window[None, :] + jax.random.normal(key_mixture, (K, ROWS), jnp.float32)
    gram_matrix = jnp.dot(mixture, mixture.T, precision=lax.Precision.HIGHEST)
    lower_factor = jnp.linalg.cholesky(gram_matrix)
    vectors = lax.linalg.triangular_solve(lower_factor, mixture, left_side=True, lower=True) * math.sqrt(ROWS)
    return (tracer, vectors.reshape(K, WZ, NX, NY))


def draw_tracer(key, part):
    return joint_draw(key)[0]


def draw_basis_vectors(key, part):
    return joint_draw(key)[1]


def block_levels(own_key, extent, cuts, smallest, largest):
    def one(dim, shards_of):
        heights = jax.random.uniform(jax.random.fold_in(jax.random.fold_in(own_key, 6), dim), (shards_of,), jnp.float32, smallest / len(cuts), largest / len(cuts))
        return jnp.repeat(jnp.exp(heights), extent[dim] // shards_of).reshape((-1,) + (1,) * (len(extent) - dim - 1))

    factor_of = one(*cuts[0])
    for cut in cuts[1:]:
        factor_of = factor_of * one(*cut)
    return factor_of


def setup_inputs(seed: int = 0) -> dict:
    key_list = jax.random.split(jax.random.key(seed), 6)
    return {
        "tracer": draw_tracer(jax.random.fold_in(key_list[5], 71), 0),
        "velocity": jnp.clip(jax.random.uniform(key_list[1], (2, NX, NY), jnp.float32, -0.25, 0.25) * block_levels(key_list[1], (2, NX, NY), ((1, 8), (2, 4)), -0.4, 0.0), -0.25, 0.25),
        "diffusivity": jnp.clip(jnp.exp(jax.random.uniform(key_list[2], (NZ,), jnp.float32, math.log(0.02), math.log(0.08))), 0.02, 0.08),
        "singular": jnp.clip(jnp.exp(jax.random.uniform(key_list[3], (K,), jnp.float32, math.log(0.5), math.log(8.0))), 0.5, 8.0),
        "basis_vectors": draw_basis_vectors(jax.random.fold_in(key_list[5], 71), 0),
    }


def advance(state, velocity, diffusivity):
    speed_x = velocity[0]
    speed_y = velocity[1]

    def level(level_index):
        centre = state[level_index]
        level_below = state[(level_index + NZ - 1) % NZ]
        level_above = state[(level_index + 1) % NZ]
        west_cells = jnp.roll(centre, 1, 0)
        east_cells = jnp.roll(centre, -1, 0)
        south_cells = jnp.roll(centre, 1, 1)
        north_cells = jnp.roll(centre, -1, 1)
        spread = west_cells + east_cells + south_cells + north_cells + level_below + level_above - 6.0 * centre
        carried = jnp.maximum(speed_x, 0.0) * (centre - west_cells) + jnp.minimum(speed_x, 0.0) * (east_cells - centre) + jnp.maximum(speed_y, 0.0) * (centre - south_cells) + jnp.minimum(speed_y, 0.0) * (north_cells - centre)
        return centre + diffusivity[level_index] * spread - carried
    return lax.map(level, jnp.arange(NZ, dtype=jnp.int32))

def upper_factor(gram_matrix):
    first_entry = jnp.sqrt(gram_matrix[0, 0])
    cross_entry = gram_matrix[0, 1] / first_entry
    second_entry = jnp.sqrt(gram_matrix[1, 1] - cross_entry * cross_entry)
    zero_entry = jnp.zeros_like(first_entry)
    return jnp.stack([jnp.stack([first_entry, cross_entry]), jnp.stack([zero_entry, second_entry])])

def orthonormal_columns(residual, factor):
    first_column = residual[0] / factor[0, 0]
    second_column = (residual[1] - factor[0, 1] * first_column) / factor[1, 1]
    return jnp.stack([first_column, second_column])

def inverse_spd(matrix):
    lower_factor = jnp.linalg.cholesky(matrix)
    identity = jnp.eye(matrix.shape[0], dtype=matrix.dtype)
    solved = lax.linalg.triangular_solve(lower_factor, identity, left_side=True, lower=True)
    return jnp.dot(solved.T, solved, precision=lax.Precision.HIGHEST)

def square_root_core(singular, projections, factor):
    vector_count = singular.shape[0]
    core_matrix = jnp.block([[jnp.diag(singular), projections], [jnp.zeros((2, vector_count), jnp.float32), factor]])
    squared = jnp.dot(core_matrix, core_matrix.T, precision=lax.Precision.HIGHEST)
    scale_factor = jnp.trace(squared) / (vector_count + 2)
    current = squared / scale_factor
    partner = jnp.eye(vector_count + 2, dtype=squared.dtype)
    for repeat in range(ROOT_ITERS):
        new_current = 0.5 * (current + inverse_spd(partner))
        new_partner = 0.5 * (partner + inverse_spd(current))
        current = 0.5 * (new_current + new_current.T)
        partner = 0.5 * (new_partner + new_partner.T)
    return jnp.sqrt(scale_factor) * current

def reference(tracer, velocity, diffusivity, singular, basis_vectors):
    after_one = advance(tracer, velocity, diffusivity)
    after_two = advance(after_one, velocity, diffusivity)
    snapshots = jnp.stack([after_one[:WZ].reshape(-1), after_two[:WZ].reshape(-1)])
    flat_basis = basis_vectors.reshape(K, -1)
    projections = jnp.dot(flat_basis, snapshots.T, precision=lax.Precision.HIGHEST) / ROWS
    residual = snapshots - jnp.dot(projections.T, flat_basis, precision=lax.Precision.HIGHEST)
    gram_matrix = jnp.dot(residual, residual.T, precision=lax.Precision.HIGHEST) / ROWS + 1e-06 * jnp.eye(2, dtype=jnp.float32)
    factor = upper_factor(gram_matrix)
    columns = orthonormal_columns(residual, factor)
    core_root = square_root_core(singular, projections, factor)
    rotated = jnp.dot(core_root[:K].T, flat_basis, precision=lax.Precision.HIGHEST) + jnp.dot(core_root[K:].T, columns, precision=lax.Precision.HIGHEST)
    return (after_two, rotated.reshape(K + 2, WZ, NX, NY))
```

```python
import math

import jax
import jax.numpy as jnp
from jax import lax
from jax.sharding import PartitionSpec as P

ROOT_ITERS = 5


def padded_2(cells, sides, width):
    for axis, dim in sides:
        count = lax.axis_size(axis)
        head = lax.slice_in_dim(cells, 0, width, axis=dim)
        tail = lax.slice_in_dim(cells, cells.shape[dim] - width, cells.shape[dim], axis=dim)
        cells = jnp.concatenate(
            [
                lax.ppermute(tail, axis, [(i, (i + 1) % count) for i in range(count)]),
                cells,
                lax.ppermute(head, axis, [((i + 1) % count, i) for i in range(count)]),
            ],
            axis=dim,
        )
    return cells


def advance(padded, velocity, diffusivity):
    centre = padded[:, 1:-1, 1:-1]
    west_cells = padded[:, :-2, 1:-1]
    east_cells = padded[:, 2:, 1:-1]
    south_cells = padded[:, 1:-1, :-2]
    north_cells = padded[:, 1:-1, 2:]
    level_below = jnp.roll(centre, 1, 0)
    level_above = jnp.roll(centre, -1, 0)
    speed_x = velocity[0]
    speed_y = velocity[1]
    spread = (
        west_cells
        + east_cells
        + south_cells
        + north_cells
        + level_below
        + level_above
        - 6.0 * centre
    )
    carried = (
        jnp.maximum(speed_x, 0.0) * (centre - west_cells)
        + jnp.minimum(speed_x, 0.0) * (east_cells - centre)
        + jnp.maximum(speed_y, 0.0) * (centre - south_cells)
        + jnp.minimum(speed_y, 0.0) * (north_cells - centre)
    )
    return centre + diffusivity[:, None, None] * spread - carried


def exchanged_step(current, velocity, diffusivity):
    padded = padded_2(current, (("gx", 1), ("gy", 2)), 1)
    return advance(padded, velocity, diffusivity)


def upper_factor(gram_matrix):
    first_entry = jnp.sqrt(gram_matrix[0, 0])
    cross_entry = gram_matrix[0, 1] / first_entry
    second_entry = jnp.sqrt(gram_matrix[1, 1] - cross_entry * cross_entry)
    zero_entry = jnp.zeros_like(first_entry)
    return jnp.stack([jnp.stack([first_entry, cross_entry]), jnp.stack([zero_entry, second_entry])])


def orthonormal_columns(residual, factor):
    first_column = residual[0] / factor[0, 0]
    second_column = (residual[1] - factor[0, 1] * first_column) / factor[1, 1]
    return jnp.stack([first_column, second_column])


def square_root_core(singular, projections, factor):
    vector_count = singular.shape[0]
    count = 2**ROOT_ITERS
    shifts = jnp.asarray([math.tan(math.pi * j / count) ** 2 for j in range(1, count // 2)], jnp.float32)
    tall = jnp.concatenate([projections, factor], axis=0)
    squares = jnp.concatenate([singular * singular, jnp.zeros((2,), jnp.float32)])
    scale_factor = (jnp.sum(squares) + jnp.sum(tall * tall)) / (vector_count + 2)
    diagonal = squares / scale_factor
    first, second = tall[:, 0] * lax.rsqrt(scale_factor), tall[:, 1] * lax.rsqrt(scale_factor)
    inverse = 1.0 / (diagonal[None, :] + shifts[:, None])
    m11 = 1.0 + jnp.sum(inverse * first * first, 1)
    m12 = jnp.sum(inverse * first * second, 1)
    m22 = 1.0 + jnp.sum(inverse * second * second, 1)
    weight = 2.0 * (1.0 + shifts) * shifts / count
    top = jnp.sqrt(weight / m11)
    ratio = m12 / m11
    low = jnp.sqrt(weight / (m22 - m12 * ratio))
    wide = jnp.concatenate(
        [
            first[None] / math.sqrt(count),
            second[None] / math.sqrt(count),
            inverse * first * top[:, None],
            inverse * (second[None] - ratio[:, None] * first[None]) * low[:, None],
        ]
    )
    straight = (1.0 + diagonal + jnp.sum((2.0 * (1.0 + shifts))[:, None] * inverse, 0) * diagonal) / count
    root = jnp.dot(wide.T, wide, precision=lax.Precision.HIGHEST) + jnp.diag(straight)
    return jnp.sqrt(scale_factor) * root


def on_device(tracer, velocity, diffusivity, singular, basis_vectors):
    vector_count = basis_vectors.shape[0]
    window = basis_vectors.shape[1]
    cells_x = basis_vectors.shape[2]
    cells_y = basis_vectors.shape[3]
    rows_all = window * cells_x * cells_y * lax.axis_size("gx") * lax.axis_size("gy")
    identity_two = jnp.eye(2, dtype=jnp.float32)
    after_one = exchanged_step(tracer, velocity, diffusivity)
    after_two = exchanged_step(after_one, velocity, diffusivity)
    snapshots = jnp.stack([after_one[:window].reshape(-1), after_two[:window].reshape(-1)])
    flat_basis = basis_vectors.reshape(vector_count, -1)
    local_products = jnp.einsum("kr,mr->km", flat_basis, snapshots, precision=lax.Precision.HIGHEST)
    local_cross = jnp.einsum("mr,nr->mn", snapshots, snapshots, precision=lax.Precision.HIGHEST)
    summed_products, summed_cross = lax.psum((local_products, local_cross), ("gx", "gy"))
    projections = summed_products / rows_all
    gram_matrix = (
        summed_cross / rows_all
        - jnp.dot(projections.T, projections, precision=lax.Precision.HIGHEST)
        + 1e-06 * identity_two
    )
    residual = snapshots - jnp.einsum(
        "km,kr->mr", projections, flat_basis, precision=lax.Precision.HIGHEST
    )
    factor = upper_factor(gram_matrix)
    columns = orthonormal_columns(residual, factor)
    core_root = square_root_core(singular, projections, factor)
    rotated = jnp.einsum(
        "ij,ir->jr", core_root[:vector_count], flat_basis, precision=lax.Precision.HIGHEST
    ) + jnp.einsum("mj,mr->jr", core_root[vector_count:], columns, precision=lax.Precision.HIGHEST)
    return (after_two, rotated.reshape(vector_count + 2, window, cells_x, cells_y))


def solution(mesh):
    return jax.shard_map(
        on_device,
        mesh=mesh,
        in_specs=(P(None, "gx", "gy"), P(None, "gx", "gy"), P(), P(), P(None, None, "gx", "gy")),
        out_specs=(P(None, "gx", "gy"), P(None, None, "gx", "gy")),
        check_vma=False,
    )
```

```python
import functools
import math

import jax
import jax.numpy as jnp
from jax import lax
from jax.experimental import pallas as pl
from jax.experimental.pallas import tpu as pltpu
from jax.sharding import PartitionSpec as P

ROOT_ITERS = 5
MESH = pl.DeviceIdType.MESH
F32 = jnp.float32
HIGHEST = lax.Precision.HIGHEST
PAD = 8
GROUP = 8


def core_root_rows(sums, singular, count_all, width):
    n = width
    k = n - 2
    lane = lax.broadcasted_iota(jnp.int32, (1, 128), 1)
    in_basis = lane < k
    total = sums * (1.0 / count_all)
    first, second = total[0:1], total[1:2]

    def pick(row, where):
        return jnp.sum(jnp.where(lane == where, row, 0.0), axis=1, keepdims=True)

    p1 = jnp.where(in_basis, first, 0.0)
    p2 = jnp.where(in_basis, second, 0.0)
    g11 = pick(first, k) - jnp.sum(p1 * p1, axis=1, keepdims=True) + 1e-6
    g12 = pick(first, k + 1) - jnp.sum(p1 * p2, axis=1, keepdims=True)
    g22 = pick(second, k + 1) - jnp.sum(p2 * p2, axis=1, keepdims=True) + 1e-6
    r11 = jnp.sqrt(g11)
    r12 = g12 / r11
    r22 = jnp.sqrt(g22 - r12 * r12)
    e1 = jnp.where(lane == k, 1.0, 0.0)
    e2 = jnp.where(lane == k + 1, 1.0, 0.0)
    v1 = p1 + r11 * e1
    v2 = p2 + r12 * e1 + r22 * e2
    squares = singular * singular
    scale = jnp.sum(squares + v1 * v1 + v2 * v2, axis=1, keepdims=True) / n
    inv_scale = 1.0 / scale
    diagonal = squares * inv_scale
    u1 = v1 * jnp.sqrt(inv_scale)
    u2 = v2 * jnp.sqrt(inv_scale)

    count = 2**ROOT_ITERS
    half = count // 2
    row = lax.broadcasted_iota(jnp.int32, (half, 1), 0)
    shifts = jnp.ones((half, 1), F32)
    for j in range(1, half):
        shifts = jnp.where(row == j - 1, math.tan(math.pi * j / count) ** 2, shifts)
    real = row < half - 1
    inverse = 1.0 / (diagonal + shifts)
    a1 = inverse * u1
    a2 = inverse * u2
    m11 = 1.0 + jnp.sum(a1 * u1, axis=1, keepdims=True)
    m12 = jnp.sum(a1 * u2, axis=1, keepdims=True)
    m22 = 1.0 + jnp.sum(a2 * u2, axis=1, keepdims=True)
    weight = 2.0 * (1.0 + shifts) / count
    ratio = m12 / m11
    top = jnp.sqrt(weight * shifts / m11)
    low = jnp.sqrt(weight * shifts / (m22 - m12 * ratio))
    z1 = jnp.where(real, a1 * top, u1 * (1.0 / math.sqrt(count)))
    z2 = jnp.where(real, (a2 - ratio * a1) * low, u2 * (1.0 / math.sqrt(count)))
    straight = (1.0 + diagonal) / count + jnp.sum(
        jnp.where(real, weight * inverse, 0.0), axis=0, keepdims=True
    ) * diagonal
    wide = jnp.concatenate([z1, z2, jnp.zeros((128 - count, 128), F32)], axis=0)
    tall = wide.T
    root = jnp.dot(tall, wide, precision=HIGHEST, preferred_element_type=F32)
    square_row = lax.broadcasted_iota(jnp.int32, (128, 128), 0)
    square_lane = lax.broadcasted_iota(jnp.int32, (128, 128), 1)
    root = (root + jnp.where(square_row == square_lane, straight, 0.0)) * jnp.sqrt(scale)
    w1 = (e1 - p1) / r11
    w2 = (e2 - p2 - r12 * w1) / r22
    mixed = jnp.where(square_lane < k, root, 0.0) + root[:, k : k + 1] * w1 + root[:, k + 1 : k + 2] * w2
    return mixed[:n, :n]


def kernel(
    nx, ny, diffusivity, velocity, singular, tracer, basis,
    out_tracer, out_basis,
    pad0, pad1, wpad, done, bas, outb, coef, acc,
    xs0, xr0, ys0, yr0, xsw, xrw, ysw, yrw, xs1, xr1, ys1, yr1,
    part, from_x, mid, from_y, spad, cmat,
    in_sem, halo_s, halo_r, gx_s, gx_r, gy_s, gy_r, out_sem, fin_sem,
):
    levels, height, lanes = tracer.shape
    k, window = basis.shape[0], basis.shape[1]
    n = k + 2
    rows = window * height
    gx, gy = lax.axis_index("gx"), lax.axis_index("gy")
    count_all = float(rows * lanes * nx * ny)

    load_tracer = pltpu.make_async_copy(tracer, pad0.at[:, PAD : PAD + height, :], in_sem.at[0])
    load_basis = pltpu.make_async_copy(basis, bas.at[:k], in_sem.at[1])
    load_tracer.start()
    load_basis.start()

    barrier = pltpu.get_barrier_semaphore()

    def greet_x(i, c):
        pl.semaphore_signal(barrier, inc=1, device_id=(lax.rem(gx + i, nx), gy), device_id_type=MESH)
        return c

    def greet_y(i, c):
        pl.semaphore_signal(barrier, inc=1, device_id=(gx, lax.rem(gy + i, ny)), device_id_type=MESH)
        return c

    lax.fori_loop(1, nx, greet_x, 0)
    lax.fori_loop(1, ny, greet_y, 0)

    vx, vy = velocity[0], velocity[1]
    coef[0] = 1.0 - jnp.abs(vx) - jnp.abs(vy)
    coef[1] = jnp.maximum(vx, 0.0)
    coef[2] = jnp.maximum(-vx, 0.0)
    coef[3] = jnp.maximum(vy, 0.0)
    coef[4] = jnp.maximum(-vy, 0.0)
    spad[...] = jnp.zeros_like(spad)
    spad[0:1, 0:k] = singular[...]
    acc[...] = jnp.zeros_like(acc)

    lane = lax.broadcasted_iota(jnp.int32, (height, lanes), 1)
    right_x, left_x = lax.rem(gx + 1, nx), lax.rem(gx + nx - 1, nx)
    right_y, left_y = lax.rem(gy + 1, ny), lax.rem(gy + ny - 1, ny)

    def halos(xs, xr, ys, yr, base):
        out = []
        for slot, (src, dst, device) in enumerate(
            [
                (xs.at[0], xr.at[0], (right_x, gy)),
                (xs.at[1], xr.at[1], (left_x, gy)),
                (ys.at[0], yr.at[0], (gx, right_y)),
                (ys.at[1], yr.at[1], (gx, left_y)),
            ]
        ):
            out.append(
                pltpu.make_async_remote_copy(
                    src_ref=src, dst_ref=dst, send_sem=halo_s.at[base + slot], recv_sem=halo_r.at[base + slot],
                    device_id=device, device_id_type=MESH,
                )
            )
        return out

    def pack(z, tile, high, low):
        here = lane == z
        return (
            jnp.where(here, pltpu.roll(tile, lax.rem(z + 1, lanes), 1), high),
            jnp.where(here, pltpu.roll(tile, z, 1), low),
        )

    def advance(centre, west, east, below, above, south_edge, north_edge, d):
        south = jnp.where(lane == 0, south_edge, pltpu.roll(centre, 1, 1))
        north = jnp.where(lane == lanes - 1, north_edge, pltpu.roll(centre, lanes - 1, 1))
        spread = (west + east) + (south + north) + (below + above)
        return (
            centre * (coef[0] - 6.0 * d)
            + (west * coef[1] + east * coef[2])
            + (south * coef[3] + north * coef[4])
            + d * spread
        )

    def edges(yr, z):
        return (
            pltpu.roll(yr[0], lax.rem(lanes - z, lanes), 1),
            pltpu.roll(yr[1], lanes - 1 - z, 1),
        )

    mid_rows = pl.ds(PAD, height)
    west_rows = pl.ds(PAD - 1, height)
    east_rows = pl.ds(PAD + 1, height)

    def level_of(src, yr, z):
        zb, za = lax.rem(z + levels - 1, levels), lax.rem(z + 1, levels)
        south_edge, north_edge = edges(yr, z)
        return advance(
            src[z, mid_rows, :], src[z, west_rows, :], src[z, east_rows, :],
            src[zb, mid_rows, :], src[za, mid_rows, :],
            south_edge, north_edge, diffusivity[z],
        )

    full = PAD + height + PAD
    flat0 = pad0.reshape(levels * full, lanes)
    flat1 = pad1.reshape(levels * full, lanes)
    zero = jnp.zeros((height, lanes), F32)

    load_tracer.wait()
    high, low = lax.fori_loop(
        0, levels, lambda z, c: pack(z, pad0[z, mid_rows, :], *c), (zero, zero), unroll=4
    )
    ys0[0], ys0[1] = high, low
    xs0[0] = flat0[pl.ds(PAD + height - 1, levels, stride=full), :]
    xs0[1] = flat0[pl.ds(PAD, levels, stride=full), :]
    pl.semaphore_wait(barrier, nx + ny - 2)
    first = halos(xs0, xr0, ys0, yr0, 0)
    for copy in first:
        copy.start()
    for copy in first:
        copy.wait_recv()
    flat0[pl.ds(PAD - 1, levels, stride=full), :] = xr0[0]
    flat0[pl.ds(PAD + height, levels, stride=full), :] = xr0[1]

    high, low = zero, zero
    for j in range(window + 2):
        z = (j - 1) % levels
        tile = level_of(pad0, yr0, z)
        wpad[j, mid_rows, :] = tile
        xsw[0, j : j + 1, :] = tile[height - 1 : height]
        xsw[1, j : j + 1, :] = tile[0:1]
        high, low = pack(j, tile, high, low)
    ysw[0], ysw[1] = high, low
    second = halos(xsw, xrw, ysw, yrw, 4)
    for copy in second:
        copy.start()

    def one(z, c):
        tile = level_of(pad0, yr0, z)
        pad1[z, mid_rows, :] = tile
        return pack(z, tile, *c)

    high, low = lax.fori_loop(0, levels, one, (zero, zero), unroll=2)
    ys1[0], ys1[1] = high, low
    xs1[0] = flat1[pl.ds(PAD + height - 1, levels, stride=full), :]
    xs1[1] = flat1[pl.ds(PAD, levels, stride=full), :]
    third = halos(xs1, xr1, ys1, yr1, 8)
    for copy in third:
        copy.start()

    for copy in second:
        copy.wait_recv()
    for j in range(1, window + 1):
        wpad[j, PAD - 1 : PAD, :] = xrw[0, j : j + 1, :]
        wpad[j, PAD + height : PAD + height + 1, :] = xrw[1, j : j + 1, :]
    load_basis.wait()
    for j in range(1, window + 1):
        south_edge, north_edge = edges(yrw, j)
        tile = advance(
            wpad[j, mid_rows, :], wpad[j, west_rows, :], wpad[j, east_rows, :],
            wpad[j - 1, mid_rows, :], wpad[j + 1, mid_rows, :],
            south_edge, north_edge, diffusivity[j - 1],
        )
        bas[k, j - 1] = wpad[j, mid_rows, :]
        bas[k + 1, j - 1] = tile

    def products(i, c):
        for m in range(2):
            total = jnp.zeros((8, lanes), F32)
            for w in range(window):
                value = bas[i, w] * bas[k + m, w]
                for r in range(height // 8):
                    total = total + value[8 * r : 8 * r + 8]
            acc[m, pl.ds(i, 1), :] = jnp.sum(total, axis=0, keepdims=True)
        return c

    lax.fori_loop(0, n, products, 0, unroll=4)
    ones = jnp.ones((8, lanes), F32)
    for m in range(2):
        row = lax.dot_general(
            ones, acc[m], (((1,), (1,)), ((), ())), precision=HIGHEST, preferred_element_type=F32
        )
        part[4 * m : 4 * m + 4, :] = row[0:4]

    def copy_x(i):
        peer = lax.rem(gx + i, nx)
        return pltpu.make_async_remote_copy(
            src_ref=part, dst_ref=from_x.at[gx], send_sem=gx_s.at[peer], recv_sem=gx_r.at[gx],
            device_id=(peer, gy), device_id_type=MESH,
        )

    def arrived_x(i):
        peer = lax.rem(gx + i, nx)
        return pltpu.make_async_remote_copy(
            src_ref=part, dst_ref=from_x.at[peer], send_sem=gx_s.at[peer], recv_sem=gx_r.at[peer],
            device_id=(peer, gy), device_id_type=MESH,
        )

    def copy_y(i):
        peer = lax.rem(gy + i, ny)
        return pltpu.make_async_remote_copy(
            src_ref=mid, dst_ref=from_y.at[gy], send_sem=gy_s.at[peer], recv_sem=gy_r.at[gy],
            device_id=(gx, peer), device_id_type=MESH,
        )

    def arrived_y(i):
        peer = lax.rem(gy + i, ny)
        return pltpu.make_async_remote_copy(
            src_ref=mid, dst_ref=from_y.at[peer], send_sem=gy_s.at[peer], recv_sem=gy_r.at[peer],
            device_id=(gx, peer), device_id_type=MESH,
        )

    def do(count, act):
        def body(i, c):
            act(i)
            return c

        lax.fori_loop(1, count, body, 0)

    from_x[gx] = part[...]
    do(nx, lambda i: copy_x(i).start())

    for copy in third:
        copy.wait_recv()
    flat1[pl.ds(PAD - 1, levels, stride=full), :] = xr1[0]
    flat1[pl.ds(PAD + height, levels, stride=full), :] = xr1[1]

    def two(z, c):
        done[z] = level_of(pad1, yr1, z)
        return c

    half = levels // 2
    lax.fori_loop(0, half, two, 0, unroll=2)
    store0 = pltpu.make_async_copy(done.at[:half], out_tracer.at[:half], out_sem.at[0])
    store0.start()

    do(nx, lambda i: arrived_x(i).wait_recv())
    total = from_x[0]
    for i in range(1, nx):
        total = total + from_x[i]
    mid[...] = total
    from_y[gy] = total
    do(ny, lambda i: copy_y(i).start())

    lax.fori_loop(half, levels, two, 0, unroll=2)
    store1 = pltpu.make_async_copy(done.at[half:], out_tracer.at[half:], out_sem.at[1])
    store1.start()

    do(ny, lambda i: arrived_y(i).wait_recv())
    total = from_y[0]
    for i in range(1, ny):
        total = total + from_y[i]
    sums = jnp.concatenate([total[0:1], total[4:5]], axis=0)
    cmat[...] = core_root_rows(sums, spad[0:1], count_all, n)

    flat_bas = bas.reshape(n * rows, lanes)
    flat_out = outb.reshape(n * rows, lanes)
    per = height // GROUP
    stores = []
    for g in range(rows // GROUP):
        def rotate(q, c):
            r = g * GROUP + 2 * q
            cols = jnp.concatenate(
                [flat_bas[pl.ds(r, n, stride=rows), :], flat_bas[pl.ds(r + 1, n, stride=rows), :]], axis=1
            )
            out = jnp.dot(cmat[...], cols, precision=HIGHEST, preferred_element_type=F32)
            flat_out[pl.ds(r, n, stride=rows), :] = out[:, :lanes]
            flat_out[pl.ds(r + 1, n, stride=rows), :] = out[:, lanes:]
            return c

        lax.fori_loop(0, GROUP // 2, rotate, 0, unroll=True)
        span = pl.ds((g % per) * GROUP, GROUP)
        store = pltpu.make_async_copy(
            outb.at[:, g // per, span, :], out_basis.at[:, g // per, span, :], fin_sem.at[g]
        )
        store.start()
        stores.append(store)

    for copy in first + second + third:
        copy.wait_send()
    do(nx, lambda i: copy_x(i).wait_send())
    do(ny, lambda i: copy_y(i).wait_send())
    store0.wait()
    store1.wait()
    for store in stores:
        store.wait()


def on_device(nx, ny, tracer, velocity, diffusivity, singular, basis_vectors):
    levels, height, lanes = tracer.shape
    k, window = basis_vectors.shape[0], basis_vectors.shape[1]
    n = k + 2
    full = PAD + height + PAD
    vmem = lambda *shape: pltpu.VMEM(shape, F32)
    dma = lambda *shape: pltpu.SemaphoreType.DMA(shape)
    any_space = pl.BlockSpec(memory_space=pl.ANY)
    return pl.pallas_call(
        functools.partial(kernel, nx, ny),
        out_shape=(
            jax.ShapeDtypeStruct((levels, height, lanes), F32),
            jax.ShapeDtypeStruct((n, window, height, lanes), F32),
        ),
        in_specs=[
            pl.BlockSpec(memory_space=pltpu.SMEM),
            pl.BlockSpec(memory_space=pltpu.VMEM),
            pl.BlockSpec(memory_space=pltpu.VMEM),
            any_space,
            any_space,
        ],
        out_specs=(any_space, any_space),
        scratch_shapes=[
            vmem(levels, full, lanes), vmem(levels, full, lanes), vmem(window + 2, full, lanes),
            vmem(levels, height, lanes), vmem(n, window, height, lanes), vmem(n, window, height, lanes),
            vmem(5, height, lanes), vmem(2, 128, lanes),
            vmem(2, levels, lanes), vmem(2, levels, lanes), vmem(2, height, lanes), vmem(2, height, lanes),
            vmem(2, 8, lanes), vmem(2, 8, lanes), vmem(2, height, lanes), vmem(2, height, lanes),
            vmem(2, levels, lanes), vmem(2, levels, lanes), vmem(2, height, lanes), vmem(2, height, lanes),
            vmem(8, lanes), vmem(nx, 8, lanes), vmem(8, lanes), vmem(ny, 8, lanes), vmem(8, 128), vmem(n, n),
            dma(2), dma(12), dma(12), dma(nx), dma(nx), dma(ny), dma(ny), dma(2), dma(window * height // GROUP),
        ],
        compiler_params=pltpu.CompilerParams(
            collective_id=0, has_side_effects=True, vmem_limit_bytes=48 * 1024 * 1024
        ),
    )(diffusivity, velocity, singular.reshape(1, k), tracer, basis_vectors)


def solution(mesh):
    return jax.shard_map(
        functools.partial(on_device, mesh.shape["gx"], mesh.shape["gy"]),
        mesh=mesh,
        in_specs=(P(None, "gx", "gy"), P(None, "gx", "gy"), P(), P(), P(None, None, "gx", "gy")),
        out_specs=(P(None, "gx", "gy"), P(None, None, "gx", "gy")),
        check_vma=False,
    )
```

```python
import functools
import math

import jax
import jax.numpy as jnp
from jax import lax
from jax.experimental import pallas as pl
from jax.experimental.pallas import tpu as pltpu
from jax.sharding import PartitionSpec as P

ROOT_ITERS = 5
MESH = pl.DeviceIdType.MESH
F32 = jnp.float32
HIGHEST = lax.Precision.HIGHEST
PAD = 8
GROUP = 8


def core_root_rows(sums, singular, count_all, width):
    n = width
    k = n - 2
    lane = lax.broadcasted_iota(jnp.int32, (1, 128), 1)
    in_basis = lane < k
    total = sums * (1.0 / count_all)
    first, second = total[0:1], total[1:2]

    def pick(row, where):
        return jnp.sum(jnp.where(lane == where, row, 0.0), axis=1, keepdims=True)

    p1 = jnp.where(in_basis, first, 0.0)
    p2 = jnp.where(in_basis, second, 0.0)
    g11 = pick(first, k) - jnp.sum(p1 * p1, axis=1, keepdims=True) + 1e-6
    g12 = pick(first, k + 1) - jnp.sum(p1 * p2, axis=1, keepdims=True)
    g22 = pick(second, k + 1) - jnp.sum(p2 * p2, axis=1, keepdims=True) + 1e-6
    r11 = jnp.sqrt(g11)
    r12 = g12 / r11
    r22 = jnp.sqrt(g22 - r12 * r12)
    e1 = jnp.where(lane == k, 1.0, 0.0)
    e2 = jnp.where(lane == k + 1, 1.0, 0.0)
    v1 = p1 + r11 * e1
    v2 = p2 + r12 * e1 + r22 * e2
    squares = singular * singular
    scale = jnp.sum(squares + v1 * v1 + v2 * v2, axis=1, keepdims=True) / n
    inv_scale = 1.0 / scale
    diagonal = squares * inv_scale
    u1 = v1 * jnp.sqrt(inv_scale)
    u2 = v2 * jnp.sqrt(inv_scale)

    count = 2**ROOT_ITERS
    half = count // 2
    row = lax.broadcasted_iota(jnp.int32, (half, 1), 0)
    shifts = jnp.ones((half, 1), F32)
    for j in range(1, half):
        shifts = jnp.where(row == j - 1, math.tan(math.pi * j / count) ** 2, shifts)
    real = row < half - 1
    inverse = 1.0 / (diagonal + shifts)
    a1 = inverse * u1
    a2 = inverse * u2
    m11 = 1.0 + jnp.sum(a1 * u1, axis=1, keepdims=True)
    m12 = jnp.sum(a1 * u2, axis=1, keepdims=True)
    m22 = 1.0 + jnp.sum(a2 * u2, axis=1, keepdims=True)
    weight = 2.0 * (1.0 + shifts) / count
    ratio = m12 / m11
    top = jnp.sqrt(weight * shifts / m11)
    low = jnp.sqrt(weight * shifts / (m22 - m12 * ratio))
    z1 = jnp.where(real, a1 * top, u1 * (1.0 / math.sqrt(count)))
    z2 = jnp.where(real, (a2 - ratio * a1) * low, u2 * (1.0 / math.sqrt(count)))
    straight = (1.0 + diagonal) / count + jnp.sum(
        jnp.where(real, weight * inverse, 0.0), axis=0, keepdims=True
    ) * diagonal
    wide = jnp.concatenate([z1, z2, jnp.zeros((128 - count, 128), F32)], axis=0)
    tall = wide.T
    root = jnp.dot(tall, wide, precision=HIGHEST, preferred_element_type=F32)
    square_row = lax.broadcasted_iota(jnp.int32, (128, 128), 0)
    square_lane = lax.broadcasted_iota(jnp.int32, (128, 128), 1)
    root = (root + jnp.where(square_row == square_lane, straight, 0.0)) * jnp.sqrt(scale)
    w1 = (e1 - p1) / r11
    w2 = (e2 - p2 - r12 * w1) / r22
    mixed = jnp.where(square_lane < k, root, 0.0) + root[:, k : k + 1] * w1 + root[:, k + 1 : k + 2] * w2
    return mixed[:n, :n]


def kernel(
    nx, ny, diffusivity, drow, velocity, singular, tracer, basis,
    out_tracer, out_basis,
    pad0, pad1, dtile, done, bas, outb, coef, acc,
    xs0, xr0, ys0, yr0, xsw, xrw, ysw, yrw, xs1, xr1, ys1, yr1,
    part, from_x, mid, from_y, spad, cmat,
    in_sem, halo_s, halo_r, gx_s, gx_r, gy_s, gy_r, out_sem, fin_sem,
):
    levels, height, lanes = tracer.shape
    k, window = basis.shape[0], basis.shape[1]
    n = k + 2
    rows = window * height
    gx, gy = lax.axis_index("gx"), lax.axis_index("gy")
    count_all = float(rows * lanes * nx * ny)

    load_tracer = pltpu.make_async_copy(tracer, pad0.at[:, PAD : PAD + height, :], in_sem.at[0])
    load_basis = pltpu.make_async_copy(basis, bas.at[:k], in_sem.at[1])
    load_tracer.start()
    load_basis.start()

    barrier = pltpu.get_barrier_semaphore()

    def greet_x(i, c):
        pl.semaphore_signal(barrier, inc=1, device_id=(lax.rem(gx + i, nx), gy), device_id_type=MESH)
        return c

    def greet_y(i, c):
        pl.semaphore_signal(barrier, inc=1, device_id=(gx, lax.rem(gy + i, ny)), device_id_type=MESH)
        return c

    lax.fori_loop(1, nx, greet_x, 0)
    lax.fori_loop(1, ny, greet_y, 0)

    vx, vy = velocity[0], velocity[1]
    coef[0] = 1.0 - jnp.abs(vx) - jnp.abs(vy)
    coef[1] = jnp.maximum(vx, 0.0)
    coef[2] = jnp.maximum(-vx, 0.0)
    coef[3] = jnp.maximum(vy, 0.0)
    coef[4] = jnp.maximum(-vy, 0.0)
    spad[...] = jnp.zeros_like(spad)
    spad[0:1, 0:k] = singular[...]
    acc[...] = jnp.zeros_like(acc)

    lane = lax.broadcasted_iota(jnp.int32, (height, lanes), 1)
    right_x, left_x = lax.rem(gx + 1, nx), lax.rem(gx + nx - 1, nx)
    right_y, left_y = lax.rem(gy + 1, ny), lax.rem(gy + ny - 1, ny)

    def halos(xs, xr, ys, yr, base):
        out = []
        for slot, (src, dst, device) in enumerate(
            [
                (xs.at[0], xr.at[0], (right_x, gy)),
                (xs.at[1], xr.at[1], (left_x, gy)),
                (ys.at[0], yr.at[0], (gx, right_y)),
                (ys.at[1], yr.at[1], (gx, left_y)),
            ]
        ):
            out.append(
                pltpu.make_async_remote_copy(
                    src_ref=src, dst_ref=dst, send_sem=halo_s.at[base + slot], recv_sem=halo_r.at[base + slot],
                    device_id=device, device_id_type=MESH,
                )
            )
        return out

    own_edge = (lane == 0) | (lane == lanes - 1)
    odd_lane = lax.rem(lane, 2) == 1
    sub = lax.broadcasted_iota(jnp.int32, (height, lanes), 0)
    mid_rows = pl.ds(PAD, height)
    west_rows = pl.ds(PAD - 1, height)
    east_rows = pl.ds(PAD + 1, height)
    full = PAD + height + PAD
    flat0 = pad0.reshape(levels * full, lanes)
    flat1 = pad1.reshape(levels * full, lanes)
    flat2 = done.reshape(levels * height, lanes)
    zero = jnp.zeros((height, lanes), F32)
    edge_zero = jnp.zeros((levels, lanes), F32)
    for flat in (flat0, flat1):
        flat[pl.ds(PAD - 1, levels, stride=full), :] = edge_zero
        flat[pl.ds(PAD + height, levels, stride=full), :] = edge_zero
    dtile[...] = jnp.broadcast_to(drow[...], (lanes, lanes)).T

    def pack(z, tile, into):
        here = (lane == z) | (lane == lax.rem(z + lanes - 1, lanes))
        return jnp.where(here, pltpu.roll(tile, z, 1), into)

    def apart(even, odd):
        low = jnp.where(odd_lane, odd, even)
        high = pltpu.roll(jnp.where(odd_lane, even, odd), 1, 1)
        return high, low

    def together(low, high):
        high = pltpu.roll(high, lanes - 1, 1)
        return jnp.where(odd_lane, high, low), jnp.where(odd_lane, low, high)

    def inner(src, z):
        d = diffusivity[z]
        zb, za = lax.rem(z + levels - 1, levels), lax.rem(z + 1, levels)
        centre = src[z, mid_rows, :]
        west, east = src[z, west_rows, :], src[z, east_rows, :]
        south = jnp.where(lane == 0, 0.0, pltpu.roll(centre, 1, 1))
        north = jnp.where(lane == lanes - 1, 0.0, pltpu.roll(centre, lanes - 1, 1))
        spread = (west + east) + (south + north) + (src[zb, mid_rows, :] + src[za, mid_rows, :])
        return (
            centre * (coef[0] - 6.0 * d)
            + (west * coef[1] + east * coef[2])
            + (south * coef[3] + north * coef[4])
            + d * spread
        )

    def add_rows(flat, begin, step, xr):
        low_row = pl.ds(begin, levels, stride=step)
        high_row = pl.ds(begin + height - 1, levels, stride=step)
        flat[low_row, :] = flat[low_row, :] + xr[0] * (coef[1, 0:1, :] + dtile[...])
        flat[high_row, :] = flat[high_row, :] + xr[1] * (coef[2, height - 1 : height, :] + dtile[...])

    def column_terms(yr):
        low = yr[0] * (coef[3][:, 0:1] + drow[...])
        high = yr[1] * (coef[4][:, lanes - 1 : lanes] + drow[...])
        return together(low, high)

    def add_columns(tile, z, terms):
        return tile + jnp.where(own_edge, pltpu.roll(terms, lax.rem(lanes - z, lanes), 1), 0.0)

    load_tracer.wait()

    def pack_pair(q, c):
        return (
            pack(2 * q, pad0[2 * q, mid_rows, :], c[0]),
            pack(2 * q + 1, pad0[2 * q + 1, mid_rows, :], c[1]),
        )

    xs0[0] = flat0[pl.ds(PAD + height - 1, levels, stride=full), :]
    xs0[1] = flat0[pl.ds(PAD, levels, stride=full), :]
    pl.semaphore_wait(barrier, nx + ny - 2)
    first = halos(xs0, xr0, ys0, yr0, 0)
    for copy in first[:2]:
        copy.start()
    ys0[0], ys0[1] = apart(*lax.fori_loop(0, levels // 2, pack_pair, (zero, zero), unroll=4))
    for copy in first[2:]:
        copy.start()

    def one(z, c):
        pad1[z, mid_rows, :] = inner(pad0, z)
        return c

    lax.fori_loop(0, levels, one, 0, unroll=8)

    for copy in first:
        copy.wait_recv()
    add_rows(flat1, PAD, full, xr0)
    terms = column_terms(yr0)

    def finish(z, parity, c):
        tile = add_columns(pad1[z, mid_rows, :], z, terms[parity])
        pad1[z, mid_rows, :] = tile
        c = list(c)
        c[parity] = pack(z, tile, c[parity])
        return tuple(c)

    packed = (zero, zero)
    for z in [levels - 1] + list(range(window + 1)):
        packed = finish(z, z % 2, packed)
    ysw[0], ysw[1] = apart(*packed)
    xsw[0] = flat1[pl.ds(PAD + height - 1, 8, stride=full), :]
    xsw[1] = flat1[pl.ds(PAD, 8, stride=full), :]
    second = halos(xsw, xrw, ysw, yrw, 4)
    for copy in second:
        copy.start()

    begin = window + 1

    def finish_pair(q, c):
        z = begin + 2 * q
        return finish(z + 1, (begin + 1) % 2, finish(z, begin % 2, c))

    packed = lax.fori_loop(0, (levels - 1 - begin) // 2, finish_pair, packed, unroll=2)
    ys1[0], ys1[1] = apart(*packed)
    xs1[0] = flat1[pl.ds(PAD + height - 1, levels, stride=full), :]
    xs1[1] = flat1[pl.ds(PAD, levels, stride=full), :]
    third = halos(xs1, xr1, ys1, yr1, 8)
    for copy in third:
        copy.start()

    def two(z, c):
        done[z] = inner(pad1, z)
        return c

    quarter, half = levels // 4, levels // 2
    lax.fori_loop(0, quarter, two, 0, unroll=8)

    load_basis.wait()
    for copy in second:
        copy.wait_recv()
    window_terms = column_terms(yrw)
    for z in range(window):
        d = diffusivity[z]
        tile = add_columns(done[z], z, window_terms[z % 2])
        tile = tile + jnp.where(sub == 0, xrw[0, z : z + 1, :] * (coef[1, 0:1, :] + d), 0.0)
        tile = tile + jnp.where(
            sub == height - 1, xrw[1, z : z + 1, :] * (coef[2, height - 1 : height, :] + d), 0.0
        )
        bas[k, z] = pad1[z, mid_rows, :]
        bas[k + 1, z] = tile

    def products(i, c):
        for m in range(2):
            total = jnp.zeros((8, lanes), F32)
            for w in range(window):
                value = bas[i, w] * bas[k + m, w]
                for r in range(height // 8):
                    total = total + value[8 * r : 8 * r + 8]
            acc[m, pl.ds(i, 1), :] = jnp.sum(total, axis=0, keepdims=True)
        return c

    lax.fori_loop(0, n, products, 0, unroll=4)
    ones = jnp.ones((8, lanes), F32)
    for m in range(2):
        row = lax.dot_general(
            ones, acc[m], (((1,), (1,)), ((), ())), precision=HIGHEST, preferred_element_type=F32
        )
        part[4 * m : 4 * m + 4, :] = row[0:4]

    def copy_x(i):
        peer = lax.rem(gx + i, nx)
        return pltpu.make_async_remote_copy(
            src_ref=part, dst_ref=from_x.at[gx], send_sem=gx_s.at[peer], recv_sem=gx_r.at[gx],
            device_id=(peer, gy), device_id_type=MESH,
        )

    def arrived_x(i):
        peer = lax.rem(gx + i, nx)
        return pltpu.make_async_remote_copy(
            src_ref=part, dst_ref=from_x.at[peer], send_sem=gx_s.at[peer], recv_sem=gx_r.at[peer],
            device_id=(peer, gy), device_id_type=MESH,
        )

    def copy_y(i):
        peer = lax.rem(gy + i, ny)
        return pltpu.make_async_remote_copy(
            src_ref=mid, dst_ref=from_y.at[gy], send_sem=gy_s.at[peer], recv_sem=gy_r.at[gy],
            device_id=(gx, peer), device_id_type=MESH,
        )

    def arrived_y(i):
        peer = lax.rem(gy + i, ny)
        return pltpu.make_async_remote_copy(
            src_ref=mid, dst_ref=from_y.at[peer], send_sem=gy_s.at[peer], recv_sem=gy_r.at[peer],
            device_id=(gx, peer), device_id_type=MESH,
        )

    def do(count, act):
        def body(i, c):
            act(i)
            return c

        lax.fori_loop(1, count, body, 0)

    from_x[gx] = part[...]
    do(nx, lambda i: copy_x(i).start())

    lax.fori_loop(quarter, half + quarter, two, 0, unroll=8)

    do(nx, lambda i: arrived_x(i).wait_recv())
    total = from_x[0]
    for i in range(1, nx):
        total = total + from_x[i]
    mid[...] = total
    from_y[gy] = total
    do(ny, lambda i: copy_y(i).start())

    lax.fori_loop(half + quarter, levels, two, 0, unroll=8)
    for copy in third:
        copy.wait_recv()
    add_rows(flat2, 0, height, xr1)
    last_terms = column_terms(yr1)

    def close_pair(q, c):
        for parity in range(2):
            z = 2 * q + parity
            done[z] = add_columns(done[z], z, last_terms[parity])
        return c

    lax.fori_loop(0, half // 2, close_pair, 0, unroll=4)
    store0 = pltpu.make_async_copy(done.at[:half], out_tracer.at[:half], out_sem.at[0])
    store0.start()
    lax.fori_loop(half // 2, half, close_pair, 0, unroll=4)
    store1 = pltpu.make_async_copy(done.at[half:], out_tracer.at[half:], out_sem.at[1])
    store1.start()

    do(ny, lambda i: arrived_y(i).wait_recv())
    total = from_y[0]
    for i in range(1, ny):
        total = total + from_y[i]
    sums = jnp.concatenate([total[0:1], total[4:5]], axis=0)
    cmat[...] = core_root_rows(sums, spad[0:1], count_all, n)

    flat_bas = bas.reshape(n * rows, lanes)
    flat_out = outb.reshape(n * rows, lanes)
    per = height // GROUP
    stores = []
    for g in range(rows // GROUP):
        def rotate(q, c):
            r = g * GROUP + 2 * q
            cols = jnp.concatenate(
                [flat_bas[pl.ds(r, n, stride=rows), :], flat_bas[pl.ds(r + 1, n, stride=rows), :]], axis=1
            )
            out = jnp.dot(cmat[...], cols, precision=HIGHEST, preferred_element_type=F32)
            flat_out[pl.ds(r, n, stride=rows), :] = out[:, :lanes]
            flat_out[pl.ds(r + 1, n, stride=rows), :] = out[:, lanes:]
            return c

        lax.fori_loop(0, GROUP // 2, rotate, 0, unroll=True)
        span = pl.ds((g % per) * GROUP, GROUP)
        store = pltpu.make_async_copy(
            outb.at[:, g // per, span, :], out_basis.at[:, g // per, span, :], fin_sem.at[g]
        )
        store.start()
        stores.append(store)

    for copy in first + second + third:
        copy.wait_send()
    do(nx, lambda i: copy_x(i).wait_send())
    do(ny, lambda i: copy_y(i).wait_send())
    store0.wait()
    store1.wait()
    for store in stores:
        store.wait()


def on_device(nx, ny, tracer, velocity, diffusivity, singular, basis_vectors):
    levels, height, lanes = tracer.shape
    k, window = basis_vectors.shape[0], basis_vectors.shape[1]
    n = k + 2
    full = PAD + height + PAD
    vmem = lambda *shape: pltpu.VMEM(shape, F32)
    dma = lambda *shape: pltpu.SemaphoreType.DMA(shape)
    any_space = pl.BlockSpec(memory_space=pl.ANY)
    return pl.pallas_call(
        functools.partial(kernel, nx, ny),
        out_shape=(
            jax.ShapeDtypeStruct((levels, height, lanes), F32),
            jax.ShapeDtypeStruct((n, window, height, lanes), F32),
        ),
        in_specs=[
            pl.BlockSpec(memory_space=pltpu.SMEM),
            pl.BlockSpec(memory_space=pltpu.VMEM),
            pl.BlockSpec(memory_space=pltpu.VMEM),
            pl.BlockSpec(memory_space=pltpu.VMEM),
            any_space,
            any_space,
        ],
        out_specs=(any_space, any_space),
        scratch_shapes=[
            vmem(levels, full, lanes), vmem(levels, full, lanes), vmem(lanes, lanes),
            vmem(levels, height, lanes), vmem(n, window, height, lanes), vmem(n, window, height, lanes),
            vmem(5, height, lanes), vmem(2, 128, lanes),
            vmem(2, levels, lanes), vmem(2, levels, lanes), vmem(2, height, lanes), vmem(2, height, lanes),
            vmem(2, 8, lanes), vmem(2, 8, lanes), vmem(2, height, lanes), vmem(2, height, lanes),
            vmem(2, levels, lanes), vmem(2, levels, lanes), vmem(2, height, lanes), vmem(2, height, lanes),
            vmem(8, lanes), vmem(nx, 8, lanes), vmem(8, lanes), vmem(ny, 8, lanes), vmem(8, 128), vmem(n, n),
            dma(2), dma(12), dma(12), dma(nx), dma(nx), dma(ny), dma(ny), dma(2), dma(window * height // GROUP),
        ],
        compiler_params=pltpu.CompilerParams(
            collective_id=0, has_side_effects=True, vmem_limit_bytes=60 * 1024 * 1024
        ),
    )(diffusivity, diffusivity.reshape(1, levels), velocity, singular.reshape(1, k), tracer, basis_vectors)


def solution(mesh):
    return jax.shard_map(
        functools.partial(on_device, mesh.shape["gx"], mesh.shape["gy"]),
        mesh=mesh,
        in_specs=(P(None, "gx", "gy"), P(None, "gx", "gy"), P(), P(), P(None, None, "gx", "gy")),
        out_specs=(P(None, "gx", "gy"), P(None, None, "gx", "gy")),
        check_vma=False,
    )
```

```python
import functools
import math

import jax
import jax.numpy as jnp
from jax import lax
from jax.experimental import pallas as pl
from jax.experimental.pallas import tpu as pltpu
from jax.sharding import PartitionSpec as P

ROOT_ITERS = 5
MESH = pl.DeviceIdType.MESH
F32 = jnp.float32
BF16 = jnp.bfloat16
HIGHEST = lax.Precision.HIGHEST
PAD = 8
GROUP = 8


def core_root_rows(sums, singular, count_all, width):
    n = width
    k = n - 2
    lane = lax.broadcasted_iota(jnp.int32, (1, 128), 1)
    in_basis = lane < k
    total = sums * (1.0 / count_all)
    first, second = total[0:1], total[1:2]

    def pick(row, where):
        return jnp.sum(jnp.where(lane == where, row, 0.0), axis=1, keepdims=True)

    p1 = jnp.where(in_basis, first, 0.0)
    p2 = jnp.where(in_basis, second, 0.0)
    g11 = pick(first, k) - jnp.sum(p1 * p1, axis=1, keepdims=True) + 1e-6
    g12 = pick(first, k + 1) - jnp.sum(p1 * p2, axis=1, keepdims=True)
    g22 = pick(second, k + 1) - jnp.sum(p2 * p2, axis=1, keepdims=True) + 1e-6
    r11 = jnp.sqrt(g11)
    r12 = g12 / r11
    r22 = jnp.sqrt(g22 - r12 * r12)
    e1 = jnp.where(lane == k, 1.0, 0.0)
    e2 = jnp.where(lane == k + 1, 1.0, 0.0)
    v1 = p1 + r11 * e1
    v2 = p2 + r12 * e1 + r22 * e2
    squares = singular * singular
    scale = jnp.sum(squares + v1 * v1 + v2 * v2, axis=1, keepdims=True) / n
    inv_scale = 1.0 / scale
    diagonal = squares * inv_scale
    u1 = v1 * jnp.sqrt(inv_scale)
    u2 = v2 * jnp.sqrt(inv_scale)

    count = 2**ROOT_ITERS
    half = count // 2
    row = lax.broadcasted_iota(jnp.int32, (half, 1), 0)
    shifts = jnp.ones((half, 1), F32)
    for j in range(1, half):
        shifts = jnp.where(row == j - 1, math.tan(math.pi * j / count) ** 2, shifts)
    real = row < half - 1
    inverse = 1.0 / (diagonal + shifts)
    a1 = inverse * u1
    a2 = inverse * u2
    m11 = 1.0 + jnp.sum(a1 * u1, axis=1, keepdims=True)
    m12 = jnp.sum(a1 * u2, axis=1, keepdims=True)
    m22 = 1.0 + jnp.sum(a2 * u2, axis=1, keepdims=True)
    weight = 2.0 * (1.0 + shifts) / count
    ratio = m12 / m11
    top = jnp.sqrt(weight * shifts / m11)
    low = jnp.sqrt(weight * shifts / (m22 - m12 * ratio))
    z1 = jnp.where(real, a1 * top, u1 * (1.0 / math.sqrt(count)))
    z2 = jnp.where(real, (a2 - ratio * a1) * low, u2 * (1.0 / math.sqrt(count)))
    straight = (1.0 + diagonal) / count + jnp.sum(
        jnp.where(real, weight * inverse, 0.0), axis=0, keepdims=True
    ) * diagonal
    wide = jnp.concatenate([z1, z2, jnp.zeros((128 - count, 128), F32)], axis=0)
    tall = wide.T
    root = jnp.dot(tall, wide, precision=HIGHEST, preferred_element_type=F32)
    square_row = lax.broadcasted_iota(jnp.int32, (128, 128), 0)
    square_lane = lax.broadcasted_iota(jnp.int32, (128, 128), 1)
    root = (root + jnp.where(square_row == square_lane, straight, 0.0)) * jnp.sqrt(scale)
    w1 = (e1 - p1) / r11
    w2 = (e2 - p2 - r12 * w1) / r22
    mixed = jnp.where(square_lane < k, root, 0.0) + root[:, k : k + 1] * w1 + root[:, k + 1 : k + 2] * w2
    return mixed[:n, :n]


def kernel(
    nx, ny, diffusivity, drow, velocity, singular, tracer, basis,
    done, bas, cmat,
    pad0, pad1, dtile, coef, acc,
    xs0, xr0, ys0, yr0, xsw, xrw, ysw, yrw, xs1, xr1, ys1, yr1,
    part, from_x, mid, from_y, spad,
    in_sem, halo_s, halo_r, gx_s, gx_r, gy_s, gy_r,
):
    levels, height, lanes = tracer.shape
    k, window = basis.shape[0], basis.shape[1]
    n = k + 2
    rows = window * height
    gx, gy = lax.axis_index("gx"), lax.axis_index("gy")
    count_all = float(rows * lanes * nx * ny)

    load_tracer = pltpu.make_async_copy(tracer, pad0.at[:, PAD : PAD + height, :], in_sem.at[0])
    load_basis = pltpu.make_async_copy(basis, bas.at[:k], in_sem.at[1])
    load_tracer.start()
    load_basis.start()

    barrier = pltpu.get_barrier_semaphore()

    def greet_x(i, c):
        pl.semaphore_signal(barrier, inc=1, device_id=(lax.rem(gx + i, nx), gy), device_id_type=MESH)
        return c

    def greet_y(i, c):
        pl.semaphore_signal(barrier, inc=1, device_id=(gx, lax.rem(gy + i, ny)), device_id_type=MESH)
        return c

    lax.fori_loop(1, nx, greet_x, 0)
    lax.fori_loop(1, ny, greet_y, 0)

    vx, vy = velocity[0], velocity[1]
    coef[0] = 1.0 - jnp.abs(vx) - jnp.abs(vy)
    coef[1] = jnp.maximum(vx, 0.0)
    coef[2] = jnp.maximum(-vx, 0.0)
    coef[3] = jnp.maximum(vy, 0.0)
    coef[4] = jnp.maximum(-vy, 0.0)
    spad[...] = jnp.zeros_like(spad)
    spad[0:1, 0:k] = singular[...]
    acc[...] = jnp.zeros_like(acc)

    lane = lax.broadcasted_iota(jnp.int32, (height, lanes), 1)
    right_x, left_x = lax.rem(gx + 1, nx), lax.rem(gx + nx - 1, nx)
    right_y, left_y = lax.rem(gy + 1, ny), lax.rem(gy + ny - 1, ny)

    def halos(xs, xr, ys, yr, base):
        out = []
        for slot, (src, dst, device) in enumerate(
            [
                (xs.at[0], xr.at[0], (right_x, gy)),
                (xs.at[1], xr.at[1], (left_x, gy)),
                (ys.at[0], yr.at[0], (gx, right_y)),
                (ys.at[1], yr.at[1], (gx, left_y)),
            ]
        ):
            out.append(
                pltpu.make_async_remote_copy(
                    src_ref=src, dst_ref=dst, send_sem=halo_s.at[base + slot], recv_sem=halo_r.at[base + slot],
                    device_id=device, device_id_type=MESH,
                )
            )
        return out

    own_edge = (lane == 0) | (lane == lanes - 1)
    odd_lane = lax.rem(lane, 2) == 1
    sub = lax.broadcasted_iota(jnp.int32, (height, lanes), 0)
    mid_rows = pl.ds(PAD, height)
    west_rows = pl.ds(PAD - 1, height)
    east_rows = pl.ds(PAD + 1, height)
    full = PAD + height + PAD
    flat0 = pad0.reshape(levels * full, lanes)
    flat1 = pad1.reshape(levels * full, lanes)
    flat2 = done.reshape(levels * height, lanes)
    zero = jnp.zeros((height, lanes), F32)
    edge_zero = jnp.zeros((levels, lanes), F32)
    for flat in (flat0, flat1):
        flat[pl.ds(PAD - 1, levels, stride=full), :] = edge_zero
        flat[pl.ds(PAD + height, levels, stride=full), :] = edge_zero
    dtile[...] = jnp.broadcast_to(drow[...], (lanes, lanes)).T

    def pack(z, tile, into):
        here = (lane == z) | (lane == lax.rem(z + lanes - 1, lanes))
        return jnp.where(here, pltpu.roll(tile, z, 1), into)

    def apart(even, odd):
        low = jnp.where(odd_lane, odd, even)
        high = pltpu.roll(jnp.where(odd_lane, even, odd), 1, 1)
        return high, low

    def together(low, high):
        high = pltpu.roll(high, lanes - 1, 1)
        return jnp.where(odd_lane, high, low), jnp.where(odd_lane, low, high)

    def inner(src, z):
        d = diffusivity[z]
        zb, za = lax.rem(z + levels - 1, levels), lax.rem(z + 1, levels)
        centre = src[z, mid_rows, :]
        west, east = src[z, west_rows, :], src[z, east_rows, :]
        south = jnp.where(lane == 0, 0.0, pltpu.roll(centre, 1, 1))
        north = jnp.where(lane == lanes - 1, 0.0, pltpu.roll(centre, lanes - 1, 1))
        spread = (west + east) + (south + north) + (src[zb, mid_rows, :] + src[za, mid_rows, :])
        return (
            centre * (coef[0] - 6.0 * d)
            + (west * coef[1] + east * coef[2])
            + (south * coef[3] + north * coef[4])
            + d * spread
        )

    def add_rows(flat, begin, step, xr):
        low_row = pl.ds(begin, levels, stride=step)
        high_row = pl.ds(begin + height - 1, levels, stride=step)
        flat[low_row, :] = flat[low_row, :] + xr[0] * (coef[1, 0:1, :] + dtile[...])
        flat[high_row, :] = flat[high_row, :] + xr[1] * (coef[2, height - 1 : height, :] + dtile[...])

    def column_terms(yr):
        low = yr[0] * (coef[3][:, 0:1] + drow[...])
        high = yr[1] * (coef[4][:, lanes - 1 : lanes] + drow[...])
        return together(low, high)

    def add_columns(tile, z, terms):
        return tile + jnp.where(own_edge, pltpu.roll(terms, lax.rem(lanes - z, lanes), 1), 0.0)

    load_tracer.wait()

    def pack_pair(q, c):
        return (
            pack(2 * q, pad0[2 * q, mid_rows, :], c[0]),
            pack(2 * q + 1, pad0[2 * q + 1, mid_rows, :], c[1]),
        )

    xs0[0] = flat0[pl.ds(PAD + height - 1, levels, stride=full), :]
    xs0[1] = flat0[pl.ds(PAD, levels, stride=full), :]
    pl.semaphore_wait(barrier, nx + ny - 2)
    first = halos(xs0, xr0, ys0, yr0, 0)
    for copy in first[:2]:
        copy.start()
    ys0[0], ys0[1] = apart(*lax.fori_loop(0, levels // 2, pack_pair, (zero, zero), unroll=4))
    for copy in first[2:]:
        copy.start()

    def one(z, c):
        pad1[z, mid_rows, :] = inner(pad0, z)
        return c

    lax.fori_loop(0, levels, one, 0, unroll=8)

    for copy in first:
        copy.wait_recv()
    add_rows(flat1, PAD, full, xr0)
    terms = column_terms(yr0)

    def finish(z, parity, c):
        tile = add_columns(pad1[z, mid_rows, :], z, terms[parity])
        pad1[z, mid_rows, :] = tile
        c = list(c)
        c[parity] = pack(z, tile, c[parity])
        return tuple(c)

    packed = (zero, zero)
    for z in [levels - 1] + list(range(window + 1)):
        packed = finish(z, z % 2, packed)
    ysw[0], ysw[1] = apart(*packed)
    xsw[0] = flat1[pl.ds(PAD + height - 1, 8, stride=full), :]
    xsw[1] = flat1[pl.ds(PAD, 8, stride=full), :]
    second = halos(xsw, xrw, ysw, yrw, 4)
    for copy in second:
        copy.start()

    begin = window + 1

    def finish_pair(q, c):
        z = begin + 2 * q
        return finish(z + 1, (begin + 1) % 2, finish(z, begin % 2, c))

    packed = lax.fori_loop(0, (levels - 1 - begin) // 2, finish_pair, packed, unroll=2)
    ys1[0], ys1[1] = apart(*packed)
    xs1[0] = flat1[pl.ds(PAD + height - 1, levels, stride=full), :]
    xs1[1] = flat1[pl.ds(PAD, levels, stride=full), :]
    third = halos(xs1, xr1, ys1, yr1, 8)
    for copy in third:
        copy.start()

    def two(z, c):
        done[z] = inner(pad1, z)
        return c

    quarter, half = levels // 4, levels // 2
    lax.fori_loop(0, quarter, two, 0, unroll=8)

    load_basis.wait()
    for copy in second:
        copy.wait_recv()
    window_terms = column_terms(yrw)
    for z in range(window):
        d = diffusivity[z]
        tile = add_columns(done[z], z, window_terms[z % 2])
        tile = tile + jnp.where(sub == 0, xrw[0, z : z + 1, :] * (coef[1, 0:1, :] + d), 0.0)
        tile = tile + jnp.where(
            sub == height - 1, xrw[1, z : z + 1, :] * (coef[2, height - 1 : height, :] + d), 0.0
        )
        bas[k, z] = pad1[z, mid_rows, :]
        bas[k + 1, z] = tile

    def products(i, c):
        for m in range(2):
            total = jnp.zeros((8, lanes), F32)
            for w in range(window):
                value = bas[i, w] * bas[k + m, w]
                for r in range(height // 8):
                    total = total + value[8 * r : 8 * r + 8]
            acc[m, pl.ds(i, 1), :] = jnp.sum(total, axis=0, keepdims=True)
        return c

    lax.fori_loop(0, n, products, 0, unroll=4)
    ones = jnp.ones((8, lanes), F32)
    for m in range(2):
        row = lax.dot_general(
            ones, acc[m], (((1,), (1,)), ((), ())), precision=HIGHEST, preferred_element_type=F32
        )
        part[4 * m : 4 * m + 4, :] = row[0:4]

    def copy_x(i):
        peer = lax.rem(gx + i, nx)
        return pltpu.make_async_remote_copy(
            src_ref=part, dst_ref=from_x.at[gx], send_sem=gx_s.at[peer], recv_sem=gx_r.at[gx],
            device_id=(peer, gy), device_id_type=MESH,
        )

    def arrived_x(i):
        peer = lax.rem(gx + i, nx)
        return pltpu.make_async_remote_copy(
            src_ref=part, dst_ref=from_x.at[peer], send_sem=gx_s.at[peer], recv_sem=gx_r.at[peer],
            device_id=(peer, gy), device_id_type=MESH,
        )

    def copy_y(i):
        peer = lax.rem(gy + i, ny)
        return pltpu.make_async_remote_copy(
            src_ref=mid, dst_ref=from_y.at[gy], send_sem=gy_s.at[peer], recv_sem=gy_r.at[gy],
            device_id=(gx, peer), device_id_type=MESH,
        )

    def arrived_y(i):
        peer = lax.rem(gy + i, ny)
        return pltpu.make_async_remote_copy(
            src_ref=mid, dst_ref=from_y.at[peer], send_sem=gy_s.at[peer], recv_sem=gy_r.at[peer],
            device_id=(gx, peer), device_id_type=MESH,
        )

    def do(count, act):
        def body(i, c):
            act(i)
            return c

        lax.fori_loop(1, count, body, 0)

    from_x[gx] = part[...]
    do(nx, lambda i: copy_x(i).start())

    lax.fori_loop(quarter, half + quarter, two, 0, unroll=8)

    do(nx, lambda i: arrived_x(i).wait_recv())
    total = from_x[0]
    for i in range(1, nx):
        total = total + from_x[i]
    mid[...] = total
    from_y[gy] = total
    do(ny, lambda i: copy_y(i).start())

    lax.fori_loop(half + quarter, levels, two, 0, unroll=8)
    for copy in third:
        copy.wait_recv()
    add_rows(flat2, 0, height, xr1)
    last_terms = column_terms(yr1)

    def close_pair(q, c):
        for parity in range(2):
            z = 2 * q + parity
            done[z] = add_columns(done[z], z, last_terms[parity])
        return c

    lax.fori_loop(0, half // 2, close_pair, 0, unroll=4)
    lax.fori_loop(half // 2, half, close_pair, 0, unroll=4)

    do(ny, lambda i: arrived_y(i).wait_recv())
    total = from_y[0]
    for i in range(1, ny):
        total = total + from_y[i]
    sums = jnp.concatenate([total[0:1], total[4:5]], axis=0)
    cmat[...] = core_root_rows(sums, spad[0:1], count_all, n)

    for copy in first + second + third:
        copy.wait_send()
    do(nx, lambda i: copy_x(i).wait_send())
    do(ny, lambda i: copy_y(i).wait_send())


def finish_kernel(done, bas, cmat, out_tracer, out_basis, outb, out_sem, fin_sem):
    n, window, height, lanes = bas.shape
    rows = window * height
    store0 = pltpu.make_async_copy(done, out_tracer, out_sem)
    store0.start()
    flat_bas = bas.reshape(n * rows, lanes)
    flat_out = outb.reshape(n * rows, lanes)
    per = height // GROUP
    coarse = cmat[...].astype(BF16)
    stacked = jnp.concatenate([coarse, (cmat[...] - coarse.astype(F32)).astype(BF16)], axis=0)
    stores = []
    for g in range(rows // GROUP):
        def rotate(q, c):
            r = g * GROUP + 2 * q
            cols = jnp.concatenate(
                [flat_bas[pl.ds(r, n, stride=rows), :], flat_bas[pl.ds(r + 1, n, stride=rows), :]], axis=1
            )
            high = cols.astype(BF16)
            rest = (cols - high.astype(F32)).astype(BF16)
            both = jnp.dot(stacked, high, preferred_element_type=F32)
            out = (jnp.dot(stacked[:n], rest, preferred_element_type=F32) + both[n:]) + both[:n]
            flat_out[pl.ds(r, n, stride=rows), :] = out[:, :lanes]
            flat_out[pl.ds(r + 1, n, stride=rows), :] = out[:, lanes:]
            return c

        lax.fori_loop(0, GROUP // 2, rotate, 0, unroll=True)
        span = pl.ds((g % per) * GROUP, GROUP)
        store = pltpu.make_async_copy(
            outb.at[:, g // per, span, :], out_basis.at[:, g // per, span, :], fin_sem.at[g]
        )
        store.start()
        stores.append(store)

    store0.wait()
    for store in stores:
        store.wait()


def on_device(nx, ny, tracer, velocity, diffusivity, singular, basis_vectors):
    levels, height, lanes = tracer.shape
    k, window = basis_vectors.shape[0], basis_vectors.shape[1]
    n = k + 2
    full = PAD + height + PAD
    vmem = lambda *shape: pltpu.VMEM(shape, F32)
    dma = lambda *shape: pltpu.SemaphoreType.DMA(shape)
    any_space = pl.BlockSpec(memory_space=pl.ANY)
    vmem_space = pl.BlockSpec(memory_space=pltpu.VMEM)
    done, bas, cmat = pl.pallas_call(
        functools.partial(kernel, nx, ny),
        out_shape=(vmem(levels, height, lanes), vmem(n, window, height, lanes), vmem(n, n)),
        in_specs=[pl.BlockSpec(memory_space=pltpu.SMEM), vmem_space, vmem_space, vmem_space, any_space, any_space],
        out_specs=(vmem_space, vmem_space, vmem_space),
        scratch_shapes=[
            vmem(levels, full, lanes), vmem(levels, full, lanes), vmem(lanes, lanes),
            vmem(5, height, lanes), vmem(2, 128, lanes),
            vmem(2, levels, lanes), vmem(2, levels, lanes), vmem(2, height, lanes), vmem(2, height, lanes),
            vmem(2, 8, lanes), vmem(2, 8, lanes), vmem(2, height, lanes), vmem(2, height, lanes),
            vmem(2, levels, lanes), vmem(2, levels, lanes), vmem(2, height, lanes), vmem(2, height, lanes),
            vmem(8, lanes), vmem(nx, 8, lanes), vmem(8, lanes), vmem(ny, 8, lanes), vmem(8, 128),
            dma(2), dma(12), dma(12), dma(nx), dma(nx), dma(ny), dma(ny),
        ],
        compiler_params=pltpu.CompilerParams(
            collective_id=0, has_side_effects=True, vmem_limit_bytes=56 * 1024 * 1024
        ),
    )(diffusivity, diffusivity.reshape(1, levels), velocity, singular.reshape(1, k), tracer, basis_vectors)
    return pl.pallas_call(
        finish_kernel,
        out_shape=(
            jax.ShapeDtypeStruct((levels, height, lanes), F32),
            jax.ShapeDtypeStruct((n, window, height, lanes), F32),
        ),
        in_specs=[vmem_space, vmem_space, vmem_space],
        out_specs=(any_space, any_space),
        scratch_shapes=[
            vmem(n, window, height, lanes), pltpu.SemaphoreType.DMA, dma(window * height // GROUP),
        ],
        compiler_params=pltpu.CompilerParams(vmem_limit_bytes=16 * 1024 * 1024),
    )(done, bas, cmat)


def solution(mesh):
    return jax.shard_map(
        functools.partial(on_device, mesh.shape["gx"], mesh.shape["gy"]),
        mesh=mesh,
        in_specs=(P(None, "gx", "gy"), P(None, "gx", "gy"), P(), P(), P(None, None, "gx", "gy")),
        out_specs=(P(None, "gx", "gy"), P(None, None, "gx", "gy")),
        check_vma=False,
    )
```
